32 devices in a mesh: dp: 8 (over y, x, core), ctx: 4 (over z).
Axes of the slice: x: 2, y: 2, z: 4, core: 2. Of those that a mesh axis runs over, the one named last changes fastest.
Arguments:
- ids: int32 [1024], P('ctx'), may hold values from 0 to 511
- tags: int32 [1024], P('ctx'), may hold values from 0 to 3
- embed: bfloat16 [512, 4096], P(None, 'dp'), may hold values from -21 to 21
- gain: float32 [4096], P('dp'), may hold values from 0.5 to 1.5
- w_in: bfloat16 [3, 4096, 4096], P(None, None, 'dp'), may hold values from -0.125 to 0.125
- short_filt: float32 [3, 7, 4096], P(None, None, 'dp'), may hold values from -2.4 to 2.4
- mr_filt: float32 [128, 4096], P(None, 'dp'), may hold values from -0.9 to 0.9
- rates: float32 [4096], P('dp'), may hold values from 0.004 to 0.12
- w_out: bfloat16 [4096, 4096], P('dp'), may hold values from -0.125 to 0.125
- w_tag: bfloat16 [4096, 4], P('dp'), may hold values from -0.25 to 0.25
Outputs:
- loss: float32 [], replicated
- block_out: bfloat16 [1024, 4096], P('ctx', 'dp')
- d_embed: float32 [512, 4096], P('ctx', 'dp')
- d_gain: float32 [4096], P('dp')
- d_w_in: float32 [3, 4096, 4096], P(None, 'ctx', 'dp')
- d_short: float32 [3, 7, 4096], P(None, None, 'dp')
- d_mr: float32 [128, 4096], P(None, 'dp')
- d_rates: float32 [4096], P('dp')
- d_w_out: float32 [4096, 4096], P('dp', 'ctx')
- d_w_tag: float32 [4096, 4], P('dp')
The draws below stay inside these ranges and needn't reach their ends.
All inputs are finite; a program needn't handle non-finite values.
Results may differ from the reference program's by a relative error of at most 0.025.
Values may be sent and summed in bfloat16 or wider, within the bound.
A program may use at most 128 MiB of HBM per device.

```python
import math
import jax
import jax.numpy as jnp
from jax import lax

D = 4096
VOCAB = 512
TAGS = 4
SHORT = 7
MEDIUM = 128
SEQ = 1024


def draw_embed(key, part):
    key_base, key_rows, key_cols = jax.random.split(key, 3)
    base = jnp.clip(jax.random.normal(key_base, (VOCAB, D), jnp.float32), -4.0, 4.0)
    row_scale = 0.3 * jnp.exp(jax.random.uniform(key_rows, (VOCAB, 1), jnp.float32, 0.0, math.log(10.0)))
    position = jnp.arange(D).astype(jnp.float32)[None, :] / D
    col_scale = 0.4 * jnp.exp(math.log(3.0) * position + 0.35 * jax.random.uniform(key_cols, (1, D), jnp.float32, -1.0, 1.0))
    return (base * row_scale * col_scale).astype(jnp.bfloat16)


def set_ends(entries, rng, smallest, high):
    longest = entries.shape.index(max(entries.shape))
    spots = []
    for shift in (0, 1):
        where = [jax.random.randint(jax.random.fold_in(rng, axis), (), 0, length) for axis, length in enumerate(entries.shape)]
        where[longest] = (where[longest] + shift) % entries.shape[longest]
        spots.append(tuple(where))
    return entries.at[spots[0]].set(smallest).at[spots[1]].set(high)


def strengthened(entries, key, source, target, shards_of, factor):
    owner, partner = [(jnp.arange(entries.shape[dim]) // (entries.shape[dim] // shards_of)).reshape([-1 if axis == dim else 1 for axis in range(entries.ndim)]) for dim in (source, target)]
    chosen = jax.random.permutation(key, shards_of)[partner]
    strong = (owner == chosen) | (owner == (partner + shards_of // 2) % shards_of)
    return jnp.where(strong, factor * entries, entries)


def steps_of(stream_key, dims, pieces, smallest, top_value):
    level = 1.0
    for dim, blocks in pieces:
        draws = jax.random.uniform(jax.random.fold_in(jax.random.fold_in(stream_key, 6), dim), (blocks,), jnp.float32, smallest / len(pieces), top_value / len(pieces))
        level = level * jnp.repeat(jnp.exp(draws), dims[dim] // blocks).reshape((-1,) + (1,) * (len(dims) - 1 - dim))
    return level


def noise(rng, dims, spread, limit, cuts=(), held_as=jnp.bfloat16):
    entries = spread * jax.random.normal(rng, dims, jnp.float32)
    if cuts:
        entries = entries * steps_of(rng, dims, cuts, -0.22, 0.18)
    return jnp.clip(entries, -limit, limit).astype(held_as)


def heavy_noise(key, shape, spread, bound, pieces, heavy, held_as=jnp.bfloat16):
    result = spread * jax.random.normal(key, shape, jnp.float32)
    if pieces:
        result = result * steps_of(key, shape, pieces, -0.22, 0.18)
    return jnp.clip(strengthened(result, jax.random.fold_in(key, 3), *heavy), -bound, bound).astype(held_as)


def setup_inputs(seed: int = 0) -> dict:
    keys = jax.random.split(jax.random.key(seed), 11)
    ids = set_ends(jax.random.randint(keys[0], (SEQ,), 0, VOCAB), jax.random.fold_in(keys[0], 1), 0, VOCAB - 1).astype(jnp.int32)
    tags = set_ends(jax.random.randint(keys[1], (SEQ,), 0, TAGS), jax.random.fold_in(keys[1], 1), 0, TAGS - 1).astype(jnp.int32)
    embed = draw_embed(jax.random.fold_in(keys[10], 71), 0)
    gain = jnp.clip(1.0 + 0.1 * jax.random.normal(keys[3], (D,), jnp.float32), 0.5, 1.5)
    w_in = heavy_noise(keys[4], (3, D, D), D ** -0.5, 0.125, ((2, 8),), (2, 1, 8, 2.0))
    short_filt = noise(keys[5], (3, SHORT, D), 0.4, 2.4, ((2, 8),), jnp.float32)
    mr_filt = noise(keys[6], (MEDIUM, D), 0.15, 0.9, ((1, 8),), jnp.float32)
    rates = jnp.clip(jnp.exp(math.log(0.12) - 3.4011973 * jax.random.uniform(keys[7], (D,), jnp.float32) ** steps_of(keys[7], (D,), ((0, 8),), -0.2, 0.2)), 0.004, 0.12)
    w_out = heavy_noise(keys[8], (D, D), D ** -0.5, 0.125, ((0, 8),), (0, 1, 8, 2.0))
    w_tag = noise(keys[9], (D, TAGS), (D // 9) ** -0.5, 0.25, ((0, 8),))
    return {"ids": ids, "tags": tags, "embed": embed, "gain": gain, "w_in": w_in, "short_filt": short_filt, "mr_filt": mr_filt, "rates": rates, "w_out": w_out, "w_tag": w_tag}


def reference(ids, tags, embed, gain, w_in, short_filt, mr_filt, rates, w_out, w_tag):
    f32 = jnp.float32
    high = lax.Precision.HIGHEST
    x0 = embed[ids]
    xf = x0.astype(f32)
    r = lax.rsqrt(lax.optimization_barrier(jnp.mean(xf * xf, axis=1, keepdims=True)) + 1e-06)
    u = (xf * r * gain[None, :]).astype(jnp.bfloat16)
    proj = jnp.stack([jnp.dot(u, w_in[j], preferred_element_type=f32) for j in range(3)]).astype(jnp.bfloat16)
    pf = proj.astype(f32)
    ppad = jnp.pad(pf, ((0, 0), (SHORT - 1, 0), (0, 0)))
    z = jnp.zeros_like(pf)
    for s in range(SHORT):
        z = z + short_filt[:, s, None, :] * ppad[:, SHORT - 1 - s:SHORT - 1 - s + SEQ, :]
    q, k, v = (z[0], z[1], z[2])
    kv = (k * v).astype(jnp.bfloat16)
    kvf = kv.astype(f32)
    lags = jnp.arange(MEDIUM).astype(f32)[:, None]
    decay = jnp.exp(-rates[None, :] * lags)
    g = mr_filt * decay
    kvpad = jnp.pad(kvf, ((MEDIUM - 1, 0), (0, 0)))

    def conv_step(s, acc):
        start = (MEDIUM - 1 - s).astype(jnp.int32)
        return acc + g[s] * lax.dynamic_slice_in_dim(kvpad, start, SEQ, 0)
    m = lax.fori_loop(jnp.int32(0), jnp.int32(MEDIUM), conv_step, jnp.zeros((SEQ, D), f32))
    h = (q * m).astype(jnp.bfloat16)
    y = jnp.dot(h, w_out, preferred_element_type=f32)
    out = xf + y
    block_out = out.astype(jnp.bfloat16)
    logits = jnp.dot(block_out, w_tag, preferred_element_type=f32)
    top = lax.optimization_barrier(jnp.max(logits, axis=1))
    lse = top + jnp.log(lax.optimization_barrier(jnp.sum(jnp.exp(logits - top[:, None]), axis=1)))
    tag_hot = (tags[:, None] == jnp.arange(TAGS)[None, :]).astype(f32)
    picked = lax.optimization_barrier(jnp.sum(logits * tag_hot, axis=1))
    loss = jnp.sum(lse - picked) / SEQ
    dlog = jnp.exp(logits - lse[:, None]) - tag_hot
    dout = jnp.dot(dlog, w_tag.astype(f32).T, precision=high)
    d_w_tag = jnp.dot(block_out.astype(f32).T, dlog, precision=high)
    dy = dout.astype(jnp.bfloat16)
    dh = jnp.dot(dy, w_out.T, preferred_element_type=f32)
    d_w_out = jnp.dot(h.T, dy, preferred_element_type=f32)
    dq = dh * m
    dm = dh * q
    dmpad = jnp.pad(dm, ((0, MEDIUM - 1), (0, 0)))

    def back_step(s, acc):
        return acc + g[s] * lax.dynamic_slice_in_dim(dmpad, s.astype(jnp.int32), SEQ, 0)
    dkv = lax.fori_loop(jnp.int32(0), jnp.int32(MEDIUM), back_step, jnp.zeros((SEQ, D), f32))

    def corr_lag(s):
        start = (MEDIUM - 1 - s).astype(jnp.int32)
        return lax.optimization_barrier(jnp.sum(dm * lax.dynamic_slice_in_dim(kvpad, start, SEQ, 0), axis=0))
    corr = lax.map(corr_lag, jnp.arange(MEDIUM).astype(jnp.int32))
    d_mr = corr * decay
    d_rates = -lax.optimization_barrier(jnp.sum(lags * mr_filt * d_mr, axis=0))
    dz = jnp.stack([dq, dkv * v, dkv * k])
    dzpad = jnp.pad(dz, ((0, 0), (0, SHORT - 1), (0, 0)))
    dp = jnp.zeros_like(dz)
    shorts = []
    for s in range(SHORT):
        dp = dp + short_filt[:, s, None, :] * dzpad[:, s:s + SEQ, :]
        shorts.append(lax.optimization_barrier(jnp.sum(dz * ppad[:, SHORT - 1 - s:SHORT - 1 - s + SEQ, :], axis=1)))
    d_short = jnp.stack(shorts, axis=1)
    dpb = dp.astype(jnp.bfloat16)
    d_w_in = jnp.stack([jnp.dot(u.T, dpb[j], preferred_element_type=f32) for j in range(3)])
    du = jnp.dot(dpb[0], w_in[0].T, preferred_element_type=f32)
    du = du + jnp.dot(dpb[1], w_in[1].T, preferred_element_type=f32)
    du = du + jnp.dot(dpb[2], w_in[2].T, preferred_element_type=f32)
    d_gain = lax.optimization_barrier(jnp.sum(du * xf * r, axis=0))
    dn = du * gain[None, :]
    row_dot = lax.optimization_barrier(jnp.mean(dn * xf, axis=1, keepdims=True))
    dx0 = dout + r * (dn - xf * r * r * row_dot)
    id_hot = (ids[:, None] == jnp.arange(VOCAB)[None, :]).astype(f32)
    d_embed = jnp.dot(id_hot.T, dx0, precision=high)
    return (loss, block_out, d_embed, d_gain, d_w_in, d_short, d_mr, d_rates, d_w_out, d_w_tag)
```

```python
import functools
import jax
import jax.numpy as jnp
from jax import lax
from jax.experimental import pallas as pl
from jax.experimental.pallas import tpu as pltpu
from jax.sharding import PartitionSpec as P

SUB = 8
LANES = 128
F32 = jnp.float32


def shifted(block, axis, distance):
    devices = range(lax.axis_size(axis))
    route = [(i - distance, i) for i in devices if i - distance in devices]
    return lax.ppermute(block, axis, route)


def rotated(block):
    n = lax.axis_size("ctx")
    return [block] + [
        lax.ppermute(block, "ctx", [(i, (i + d) % n) for i in range(n)]) for d in range(1, n)
    ]


def sublanes():
    return lax.broadcasted_iota(jnp.int32, (SUB, LANES), 0)


def row(ref, i):
    return jnp.broadcast_to(ref[pl.ds(i, 1), :], (SUB, LANES))


def fill_taps(ext, block, halo, taps, count):
    first = sublanes() < 1
    for i in range(taps - 1):
        rolled = pltpu.roll(block[count - (taps - 1) + i], 1, 0)
        ext[i] = jnp.where(first, row(halo, i), rolled)
    for a in range(count):
        ext[taps - 1 + a] = block[a]


def fill_back(ext, kv, halo, span, count):
    sub = sublanes()
    for a in range(count):
        tile, before = kv[a], halo[a]
        ext[span + a] = tile
        for k in range(1, span // count + 1):
            ext[span - count * k + a] = jnp.where(
                sub < k, pltpu.roll(before, k, 0), pltpu.roll(tile, k, 0)
            )


def forward_kernel(p0, p1, p2, a0, a1, a2, sf, g3, kvh, q, k, v, kv, m, h, pe, kve):
    count, taps, span = p0.shape[0], sf.shape[1], g3.shape[0]
    for j, (block, halo, out) in enumerate(((p0, a0, q), (p1, a1, k), (p2, a2, v))):
        fill_taps(pe, block, halo, taps, count)
        weights = [row(sf.at[j], s) for s in range(taps)]
        for a in range(count):
            total = weights[0] * pe[taps - 1 + a]
            for s in range(1, taps):
                total = total + weights[s] * pe[taps - 1 + a - s]
            out[a] = total
    for a in range(count):
        kv[a] = (k[a] * v[a]).astype(jnp.bfloat16).astype(F32)
    fill_back(kve, kv, kvh, span, count)
    half, step = count // 2, 8
    for part in range(2):
        base = part * half

        def lags(c, acc):
            s0 = c * step
            start = span + base - s0 - (step - 1)
            tiles = [kve[start + i] for i in range(half + step - 1)]
            acc = list(acc)
            for i in range(step):
                w = g3[s0 + i]
                for a in range(half):
                    acc[a] = acc[a] + w * tiles[a + step - 1 - i]
            return tuple(acc)

        acc = lax.fori_loop(0, span // step, lags, (jnp.zeros((SUB, LANES), F32),) * half)
        for a in range(half):
            m[base + a] = acc[a]
    h[...] = (q[...] * m[...]).reshape(h.shape).astype(jnp.bfloat16)


def backward_kernel(
    dh, dhh, qh, h6, q, k, v, m, kv, kvh, p0, p1, p2, a0, a1, a2, sf, g3,
    d0, d1, d2, corr, short, kve, dme, dke, dze, pe, dpo,
):
    count, taps, span = p0.shape[0], sf.shape[1], g3.shape[0]
    sub = sublanes()
    fill_back(kve, kv, kvh, span, count)
    for a in range(count):
        tile = dh[a] * q[a]
        after = dhh[a] * qh[a]
        dme[a] = tile
        for n in range(1, span // count + 2):
            if n * count + a < dme.shape[0]:
                dme[n * count + a] = jnp.where(
                    sub < SUB - n, pltpu.roll(tile, SUB - n, 0), pltpu.roll(after, SUB - n, 0)
                )
    step = 8
    half = (count + taps - 1) // 2
    for part in range(2):
        base = part * half

        def lags(c, acc):
            s0 = c * step
            tiles = [dme[base + s0 + i] for i in range(half + step - 1)]
            acc = list(acc)
            for i in range(step):
                w = g3[s0 + i]
                for a in range(half):
                    acc[a] = acc[a] + w * tiles[a + i]
            return tuple(acc)

        acc = lax.fori_loop(0, span // step, lags, (jnp.zeros((SUB, LANES), F32),) * half)
        for a in range(half):
            dke[base + a] = acc[a]

    def corr_lags(c, carry):
        s0 = c * step
        start = span - s0 - (step - 1)
        acc = [jnp.zeros((SUB, LANES), F32)] * step
        for a in range(count):
            w = dme[a]
            for i in range(step):
                acc[i] = acc[i] + w * kve[start + a + step - 1 - i]
        for i in range(step):
            corr[s0 + i] = acc[i]
        return carry

    lax.fori_loop(0, span // step, corr_lags, 0)
    last = sub >= SUB - 1
    for j, (block, halo, out) in enumerate(((p0, a0, d0), (p1, a1, d1), (p2, a2, d2))):
        other = (m, v, k)[j]
        for a in range(count):
            dze[a] = (dh[a] if j == 0 else dke[a]) * other[a]
        for a in range(taps - 1):
            tail = jnp.where(last, row(h6.at[j], a), pltpu.roll(other[a], SUB - 1, 0))
            if j == 0:
                grad = jnp.where(last, pltpu.roll(dhh[a], SUB - 1, 0), pltpu.roll(dh[a], SUB - 1, 0))
            else:
                grad = dke[count + a]
            dze[count + a] = grad * tail
        fill_taps(pe, block, halo, taps, count)
        weights = [row(sf.at[j], s) for s in range(taps)]
        sums = [jnp.zeros((SUB, LANES), F32)] * taps
        for a in range(count):
            total = weights[0] * dze[a]
            mine = dze[a]
            for s in range(1, taps):
                total = total + weights[s] * dze[a + s]
            for s in range(taps):
                sums[s] = sums[s] + mine * pe[taps - 1 + a - s]
            dpo[a] = total
        out[...] = dpo[...].reshape(out.shape).astype(jnp.bfloat16)
        for s in range(taps):
            short[j * taps + s] = sums[s]


def tiles_spec(lead, offset=0):
    return pl.BlockSpec((lead, SUB, LANES), lambda i: (0, 0, i + offset))


def rows_spec(lead, offset=0):
    return pl.BlockSpec((lead, LANES), lambda i: (0, i + offset))


def body(ids, tags, embed, gain, w_in, short_filt, mr_filt, rates, w_out, w_tag):
    high = lax.Precision.HIGHEST
    bf16 = jnp.bfloat16
    rows = ids.shape[0]
    count = rows // SUB
    vocab, slab = embed.shape
    width = w_in.shape[1]
    n_tags = w_tag.shape[1]
    taps = short_filt.shape[1]
    span = mr_filt.shape[0]
    n_ctx = lax.axis_size("ctx")
    c = lax.axis_index("ctx")
    share = width // n_ctx
    blocks = slab // LANES

    def natural(x):
        return x.reshape(x.shape[:-1] + (count, SUB)).swapaxes(-1, -2).reshape(x.shape)

    def woven(x):
        return x.reshape(SUB, count).swapaxes(0, 1).reshape(rows)

    ids_w, tags_w = woven(ids), woven(tags)
    lanes = jnp.arange(vocab)[None, :]
    id_hot = (ids_w[:, None] == lanes).astype(bf16)
    id_nat = (ids[:, None] == lanes).astype(bf16)
    xs = jnp.dot(id_hot, embed, preferred_element_type=F32)
    x_full = lax.all_gather(xs.astype(bf16), "dp", axis=1, tiled=True)
    tag_slab = w_tag.astype(F32).T
    small = lax.all_gather(jnp.concatenate([gain[None], tag_slab]), "dp", axis=1, tiled=True)
    gain_full, tag_full = small[0], small[1:]
    lags = jnp.arange(span).astype(F32)[:, None]
    decay = jnp.exp(-rates[None, :] * lags)
    g3 = jnp.broadcast_to((mr_filt * decay)[:, None, :], (span, SUB, slab))
    head = lax.dot_general(
        tag_full.astype(bf16), w_out, (((1,), (1,)), ((), ())), preferred_element_type=F32
    )
    x_full, table = lax.optimization_barrier((x_full, embed))
    table = lax.all_gather(table, "dp", axis=1, tiled=True)
    ids_all = jnp.concatenate(rotated(ids_w.astype(F32))).astype(jnp.int32)
    xf = x_full.astype(F32)
    r = lax.rsqrt(jnp.sum(xf * xf, axis=1, keepdims=True) / width + 1e-06)
    u = (xf * r * gain_full[None, :]).astype(bf16)
    pb = [jnp.dot(u, w_in[j], preferred_element_type=F32).astype(bf16) for j in range(3)]
    proj = jnp.concatenate(pb, axis=1).reshape(count, SUB, 3 * slab)
    pf = proj.astype(F32)
    edge = shifted(proj[count - (taps - 1) :, SUB - 1, :], "ctx", 1).astype(F32)
    keep = span // count
    late = jnp.concatenate(
        [pf[count - (taps - 1) :, SUB - 1 - keep : SUB - 1], pf[:, SUB - keep :]], axis=0
    )
    zt = []
    for j in (1, 2):
        src = late[:, :, j * slab : (j + 1) * slab]
        zt.append(
            sum(short_filt[j, s] * src[taps - 1 - s : taps - 1 - s + count] for s in range(taps))
        )
    kv_tail = (zt[0] * zt[1]).astype(bf16)
    kvh = shifted(kv_tail, "ctx", 1).astype(F32)
    kvh = jnp.pad(kvh, ((0, 0), (SUB - keep, 0), (0, 0)))

    tile_out = jax.ShapeDtypeStruct((count, SUB, slab), F32)
    flat_out = jax.ShapeDtypeStruct((rows, slab), bf16)
    p_specs = [tiles_spec(count, j * blocks) for j in range(3)]
    a_specs = [rows_spec(taps - 1, j * blocks) for j in range(3)]
    sf_spec = pl.BlockSpec((3, taps, LANES), lambda i: (0, 0, i))
    q, k, v, kv, m, h = pl.pallas_call(
        forward_kernel,
        grid=(blocks,),
        in_specs=p_specs + a_specs + [sf_spec, tiles_spec(span), tiles_spec(count)],
        out_specs=[tiles_spec(count)] * 5 + [rows_spec(rows)],
        out_shape=[tile_out] * 5 + [flat_out],
        scratch_shapes=[
            pltpu.VMEM((count + taps - 1, SUB, LANES), F32),
            pltpu.VMEM((span + count, SUB, LANES), F32),
        ],
        compiler_params=pltpu.CompilerParams(vmem_limit_bytes=40 * 2**20),
        cost_estimate=pl.CostEstimate(
            flops=2 * rows * slab * span, bytes_accessed=8 * 2**20, transcendentals=0
        ),
        name="mix_forward",
    )(pf, pf, pf, edge, edge, edge, short_filt, g3, kvh)

    ahead = keep + 1
    qh = shifted(q[:, :ahead].astype(bf16), "ctx", -1).astype(F32)
    qh = jnp.pad(qh, ((0, 0), (0, SUB - ahead), (0, 0)))
    h6 = shifted(jnp.stack([x[: taps - 1, 0] for x in (m, v, k)]), "ctx", -1)

    part = lax.dot_general(
        w_tag, xs.astype(bf16), (((0,), (1,)), ((), ())), preferred_element_type=F32
    ) + lax.dot_general(head, h.astype(F32), (((1,), (1,)), ((), ())), precision=high)
    logits = lax.psum(part, "dp")
    top = jnp.max(logits, axis=0)
    lse = top + jnp.log(jnp.sum(jnp.exp(logits - top[None]), axis=0))
    tag_hot = (tags_w[None, :] == jnp.arange(n_tags)[:, None]).astype(F32)
    loss_part = jnp.sum(lse - jnp.sum(logits * tag_hot, axis=0))
    dlog = jnp.exp(logits - lse[None]) - tag_hot
    dlog_h = shifted(dlog, "ctx", -1)
    mixed = (((0,), (0,)), ((), ()))
    dh = lax.dot_general(dlog, head, mixed, precision=high)
    dhh = lax.dot_general(dlog_h, head, mixed, precision=high)

    spot = jnp.arange(rows)
    where = (spot % count) * SUB + spot // count
    weave = (where[:, None] == spot[None, :]).astype(bf16)
    h_late, _, table = lax.optimization_barrier((h, logits, table))
    h_nat = jnp.dot(weave, h_late, preferred_element_type=F32).astype(bf16)
    y_part = jnp.dot(h_nat, w_out, preferred_element_type=F32).astype(bf16)
    y_part, dh = lax.optimization_barrier((y_part, dh))
    y = lax.psum_scatter(y_part, "dp", scatter_dimension=1, tiled=True)
    out_part = jnp.dot(dlog, h.astype(F32), precision=high)

    d0, d1, d2, corr8, short8 = pl.pallas_call(
        backward_kernel,
        grid=(blocks,),
        in_specs=[tiles_spec(count)] * 3
        + [pl.BlockSpec((3, taps - 1, LANES), lambda i: (0, 0, i))]
        + [tiles_spec(count)] * 6
        + p_specs
        + a_specs
        + [sf_spec, tiles_spec(span)],
        out_specs=[rows_spec(rows)] * 3 + [tiles_spec(span), tiles_spec(3 * taps)],
        out_shape=[flat_out] * 3
        + [
            jax.ShapeDtypeStruct((span, SUB, slab), F32),
            jax.ShapeDtypeStruct((3 * taps, SUB, slab), F32),
        ],
        scratch_shapes=[
            pltpu.VMEM((span + count, SUB, LANES), F32),
            pltpu.VMEM((span + count + taps - 1, SUB, LANES), F32),
            pltpu.VMEM((count + taps - 1, SUB, LANES), F32),
            pltpu.VMEM((count + taps - 1, SUB, LANES), F32),
            pltpu.VMEM((count + taps - 1, SUB, LANES), F32),
            pltpu.VMEM((count, SUB, LANES), F32),
        ],
        compiler_params=pltpu.CompilerParams(vmem_limit_bytes=40 * 2**20),
        cost_estimate=pl.CostEstimate(
            flops=4 * rows * slab * span, bytes_accessed=12 * 2**20, transcendentals=0
        ),
        name="mix_backward",
    )(
        dh.reshape(count, SUB, slab), dhh.reshape(count, SUB, slab), qh, h6, q, k, v, m, kv, kvh,
        pf, pf, pf, edge, edge, edge, short_filt, g3,
    )

    dpb = jnp.concatenate([d0, d1, d2], axis=1)
    dp_parts = rotated(dpb)[1:]

    y, e1, e2 = lax.optimization_barrier((y, d1, d2))
    across = (((1,), (1,)), ((), ()))
    du_part = sum(
        lax.dot_general(g, w_in[j], across, preferred_element_type=F32)
        for j, g in enumerate((d0, e1, e2))
    )
    du_part, dp_parts[0], table, d0, d1, d2 = lax.optimization_barrier(
        (du_part.astype(bf16), dp_parts[0], table, d0, d1, d2)
    )
    du = lax.psum_scatter(du_part, "dp", scatter_dimension=1, tiled=True)
    du, *dp_parts = lax.optimization_barrier((du, *dp_parts))
    du = du.astype(F32)
    dp_all = jnp.concatenate([dpb, *dp_parts], axis=0)
    x_nat = jnp.dot(id_nat, embed, preferred_element_type=F32)
    block_out = (x_nat + y.astype(F32)).astype(bf16)
    tag_part = jnp.dot(natural(dlog), block_out.astype(F32), precision=high)
    tf = table.astype(F32)
    r_word = lax.rsqrt(jnp.sum(tf * tf, axis=1, keepdims=True) / width + 1e-06)
    gain_mine = lax.dynamic_slice_in_dim(gain_full, c * share, share, 0)
    t_mine = lax.dynamic_slice_in_dim(table, c * share, share, 1).astype(F32)
    u_word = (t_mine * r_word * gain_mine[None, :]).astype(bf16)
    hot_all = (ids_all[:, None] == lanes).astype(bf16)
    u_all = jnp.dot(hot_all, u_word, preferred_element_type=F32).astype(bf16)

    inner = sum(
        jnp.sum(g.astype(F32) * x.astype(F32), axis=1) for g, x in zip((d0, d1, d2), pb)
    )
    row_dot = lax.psum(inner, "dp")[:, None] / (r * width)

    sums = jnp.concatenate(
        [jnp.sum(corr8, axis=1), jnp.sum(short8, axis=1), tag_part, out_part,
         jnp.full((1, slab), loss_part)], axis=0
    )
    sums, _ = lax.optimization_barrier((sums.astype(bf16), du))
    sums = sum(x.astype(F32) for x in rotated(sums))
    ends = [span, span + 3 * taps, span + 3 * taps + n_tags, span + 3 * taps + 2 * n_tags]
    d_mr = sums[: ends[0]] * decay
    d_short = sums[ends[0] : ends[1]].reshape(3, taps, slab)
    d_w_tag = sums[ends[1] : ends[2]].T
    d_rates = -jnp.sum(lags * mr_filt * d_mr, axis=0)
    loss = sums[ends[3], 0] / (rows * n_ctx)
    tag_mine = lax.dynamic_slice_in_dim(tag_full, c * share, share, 1)
    d_w_out = lax.dot_general(sums[ends[2] : ends[3]], tag_mine, mixed, precision=high)

    dn = du * gain[None, :]
    gain_part = jnp.sum(du * xs * r, axis=0)
    dout = lax.dot_general(dlog, tag_slab, mixed, precision=high)
    dx0 = dout + r * (dn - xs * r * r * row_dot)
    hi = dx0.astype(bf16)
    lo = (dx0 - hi.astype(F32)).astype(bf16)
    embed_part = lax.dot_general(id_hot, hi, mixed, preferred_element_type=F32) + lax.dot_general(
        id_hot, lo, mixed, preferred_element_type=F32
    )
    per = vocab // n_ctx
    extra = jnp.broadcast_to(gain_part, (n_ctx, SUB * 2, slab))
    packed = jnp.concatenate([embed_part.reshape(n_ctx, per, slab), extra], axis=1)
    packed = packed.reshape(n_ctx * (per + SUB * 2), slab).astype(bf16)
    mine = lax.psum_scatter(packed, "ctx", scatter_dimension=0, tiled=True).astype(F32)
    d_embed, d_gain = mine[:per], mine[per]

    d_w_in = jnp.stack(
        [
            lax.dot_general(
                u_all, dp_all[:, j * slab : (j + 1) * slab], mixed, preferred_element_type=F32
            )
            for j in range(3)
        ]
    )
    return (loss, block_out, d_embed, d_gain, d_w_in, d_short, d_mr, d_rates, d_w_out, d_w_tag)


def solution(mesh):
    placed = (
        P("ctx"),
        P("ctx"),
        P(None, "dp"),
        P("dp"),
        P(None, None, "dp"),
        P(None, None, "dp"),
        P(None, "dp"),
        P("dp"),
        P("dp", None),
        P("dp", None),
    )
    return jax.shard_map(
        body,
        mesh=mesh,
        in_specs=placed,
        out_specs=(
            P(),
            P("ctx", "dp"),
            P("ctx", "dp"),
            P("dp"),
            P(None, "ctx", "dp"),
            P(None, None, "dp"),
            P(None, "dp"),
            P("dp"),
            P("dp", "ctx"),
            P("dp", None),
        ),
        check_vma=False,
    )
```
